256 devices in a mesh: mem: 64 (over y, z, core), blk: 4 (over x).
Axes of the slice: x: 4, y: 4, z: 8, core: 2. Of those that a mesh axis runs over, the one named last changes fastest.
Arguments:
- queries: bfloat16 [32768, 2048], P('mem', 'blk'), may hold values from -40 to 40
- local_keys: bfloat16 [32768, 2048], P('mem', 'blk'), may hold values from -6 to 7
- local_values: bfloat16 [32768, 2048], P('mem', 'blk'), may hold values from -6 to 6
- memory_keys: bfloat16 [256, 128, 2048], P('mem', None, 'blk'), may hold values from -6 to 7
- memory_values: bfloat16 [256, 128, 2048], P('mem', None, 'blk'), may hold values from -6 to 6
- block_ids: int32 [256, 8], P('mem'), may hold values from 0 to 255, as said below
- gate_index: int32 [16], P('blk'), may hold values from 0 to 3
- gate_vectors: float32 [4, 128], replicated, may hold values from -6 to 6
- out_weight: bfloat16 [2048, 4096], P(None, 'blk'), may hold values from -0.125 to 0.125
Outputs:
- mixed: bfloat16 [32768, 4096], P('mem', 'blk')
The draws below stay inside these ranges and needn't reach their ends.
Inputs may be any that keep to these rules, and one draw needn't show every extreme that they name: `block_ids`: block id i is kept by owner i // 4. The 8 ids of one query block have different owners; the ids of the 4 query blocks of one index of mem are all different, name at most 1 block of any one owner, and name exactly 1 block of some owner.
All inputs are finite; a program needn't handle non-finite values.
Results may differ from the reference program's by a relative error of at most 0.015.
Values may be sent and summed in bfloat16 or wider, within the bound.
No kernel may reach another device: no remote copies, remote signals or barrier semaphores. Data moves between devices by JAX's collectives and lax.ppermute only.
A program may use at most 128 MiB of HBM per device.

```python
import jax
import jax.numpy as jnp
from jax import lax

D = 4096
HEADS = 16
HD = 128
BT = 128
TOPK = 8
NGATE = 4
QB_DEV = 4
MEMB_DEV = 4
TOKENS = 32768
MEMB = 256
N_MEM = 64


def draw_queries(key, part):
    key = jax.random.fold_in(key, 11)
    values = jnp.clip(jax.random.normal(jax.random.fold_in(key, 1), (TOKENS, HEADS * HD), jnp.float32), -6.0, 6.0)
    return values.astype(jnp.bfloat16)


def draw_local_keys(key, part):
    key = jax.random.fold_in(key, 12)
    values = jnp.clip(jax.random.normal(key, (TOKENS, HEADS * HD), jnp.float32), -6.0, 6.0)
    return values.astype(jnp.bfloat16)


def draw_memory_keys(key, part):
    key = jax.random.fold_in(key, 13)
    values = jnp.clip(jax.random.normal(key, (MEMB, BT, HEADS * HD), jnp.float32), -6.0, 6.0)
    return values.astype(jnp.bfloat16)


def draw_block_ids(key, part):
    key = jax.random.fold_in(key, 14)
    hotness = jax.random.randint(jax.random.fold_in(key, 1), (N_MEM,), 0, 4)
    noise = jax.random.randint(jax.random.fold_in(key, 2), (N_MEM, N_MEM), 0, 1024)
    owners = jnp.arange(N_MEM, dtype=jnp.int32)
    score = (hotness[None, :] * 1024 + noise) * N_MEM + owners[None, :]
    unused, order = lax.top_k(score, N_MEM)
    wanted = QB_DEV * TOPK
    rank = jnp.arange(wanted, dtype=jnp.int32)
    owner = order[:, rank % N_MEM].astype(jnp.int32)
    copy = rank // N_MEM
    offset = jax.random.randint(jax.random.fold_in(key, 3), (N_MEM, N_MEM), 0, MEMB_DEV)
    chosen = jnp.take_along_axis(offset, owner, axis=1)
    local = (chosen + copy[None, :]) % MEMB_DEV
    ids = owner * MEMB_DEV + local
    return ids.reshape(N_MEM * QB_DEV, TOPK).astype(jnp.int32)


def plant(entries, key, smallest, top_value):
    extent = entries.shape
    spot = [jax.random.randint(jax.random.fold_in(key, axis), (), 0, extent[axis]) for axis in range(len(extent))]
    entries = entries.at[tuple(spot)].set(smallest)
    longest = extent.index(max(extent))
    spot[longest] = (spot[longest] + 1) % extent[longest]
    return entries.at[tuple(spot)].set(top_value)


def block_levels(key, extent, shards, low, largest):
    factor_of, own = 1.0, jax.random.fold_in(key, 6)
    for position, blocks in shards:
        draws = jnp.exp(jax.random.uniform(jax.random.fold_in(own, position), (blocks,), jnp.float32, low / len(shards), largest / len(shards)))
        factor_of = factor_of * jnp.repeat(draws, extent[position] // blocks).reshape([-1 if axis == position else 1 for axis in range(len(extent))])
    return factor_of


def gaussian(rng, dims, spread, reach, split=(), kind=jnp.bfloat16):
    values = jax.random.normal(rng, dims, jnp.float32) * spread
    if len(split) > 0:
        values = block_levels(rng, dims, split, -0.22, 0.18) * values
    return jnp.clip(values, min=-reach, max=reach).astype(kind)


def setup_inputs(seed: int = 0) -> dict:
    key_of = jax.random.split(jax.random.key(seed), 10)
    return {
        "queries": draw_queries(jax.random.fold_in(key_of[9], 71), 0),
        "local_keys": draw_local_keys(jax.random.fold_in(key_of[9], 71), 0),
        "local_values": gaussian(key_of[2], (TOKENS, HEADS * HD), 1.0, 6.0, ((0, 64), (1, 4))),
        "memory_keys": draw_memory_keys(jax.random.fold_in(key_of[9], 71), 0),
        "memory_values": gaussian(key_of[4], (MEMB, BT, HEADS * HD), 1.0, 6.0, ((0, 64), (2, 4))),
        "block_ids": draw_block_ids(jax.random.fold_in(key_of[9], 71), 0),
        "gate_index": plant(jax.random.randint(key_of[6], (HEADS,), 0, NGATE), jax.random.fold_in(key_of[6], 1), 0, NGATE - 1).astype(jnp.int32),
        "gate_vectors": gaussian(key_of[7], (NGATE, HD), 1.5, 6.0, (), jnp.float32),
        "out_weight": gaussian(key_of[8], (HEADS * HD, D), (HEADS * HD) ** -0.5, 0.125, ((1, 4),)),
    }


def attend(queries, keys, values, allowed, scale):
    scores = jnp.einsum("bqhd,bkhd->bhqk", queries.astype(jnp.float32), keys.astype(jnp.float32)) * scale
    scores = jnp.where(allowed, scores, jnp.float32(-1e30))
    top = jnp.max(scores, axis=-1, keepdims=True)
    weights = jnp.exp(scores - top)
    probs = (weights / jnp.sum(weights, axis=-1, keepdims=True)).astype(jnp.bfloat16)
    return jnp.einsum("bhqk,bkhd->bqhd", probs.astype(jnp.float32), values.astype(jnp.float32))


def reference(queries, local_keys, local_values, memory_keys, memory_values, block_ids, gate_index, gate_vectors, out_weight):
    scale = float(HD) ** -0.5
    tok_dev = QB_DEV * BT
    gate_rows = gate_vectors[gate_index]

    def shard(index):
        start = index * tok_dev
        before = jnp.maximum(start - tok_dev, 0)
        heads_q = lax.dynamic_slice_in_dim(queries, start, tok_dev, 0).reshape(tok_dev, HEADS, HD)
        keys = jnp.concatenate([lax.dynamic_slice_in_dim(local_keys, before, tok_dev, 0), lax.dynamic_slice_in_dim(local_keys, start, tok_dev, 0)], axis=0)
        values = jnp.concatenate([lax.dynamic_slice_in_dim(local_values, before, tok_dev, 0), lax.dynamic_slice_in_dim(local_values, start, tok_dev, 0)], axis=0)
        rows = jnp.arange(tok_dev, dtype=jnp.int32)[:, None]
        cols = jnp.arange(2 * tok_dev, dtype=jnp.int32)[None, :]
        allowed = (cols > rows) & (cols <= rows + tok_dev) & ((cols >= tok_dev) | (index > 0))
        local_out = attend(heads_q[None], keys.reshape(1, 2 * tok_dev, HEADS, HD), values.reshape(1, 2 * tok_dev, HEADS, HD), allowed[None, None], scale)[0]
        ids = lax.dynamic_slice_in_dim(block_ids, index * QB_DEV, QB_DEV, 0).reshape(-1)
        mem_k = memory_keys[ids].reshape(QB_DEV, TOPK * BT, HEADS, HD)
        mem_v = memory_values[ids].reshape(QB_DEV, TOPK * BT, HEADS, HD)
        open_mask = jnp.ones((1, 1, BT, TOPK * BT), dtype=bool)
        memory_out = attend(heads_q.reshape(QB_DEV, BT, HEADS, HD), mem_k, mem_v, open_mask, scale).reshape(tok_dev, HEADS, HD)
        logits = jnp.einsum("thd,hd->th", heads_q.astype(jnp.float32), gate_rows, precision=lax.Precision.HIGHEST) * scale
        gate = jax.nn.sigmoid(logits)[:, :, None]
        attended = (gate * memory_out + (1.0 - gate) * local_out).astype(jnp.bfloat16).reshape(tok_dev, HEADS * HD)
        return jnp.dot(attended, out_weight, preferred_element_type=jnp.float32).astype(jnp.bfloat16)

    return lax.map(shard, jnp.arange(N_MEM, dtype=jnp.int32)).reshape(TOKENS, D)
```

```python
import functools

import jax
import jax.numpy as jnp
from jax import lax
from jax.experimental import pallas as pl
from jax.experimental.pallas import tpu as pltpu
from jax.sharding import PartitionSpec as P

NY, NZ, NC, NX = 4, 8, 2, 4
HD = 128
BT = 128
TOK = 512
NH = 4
QB = 4
SLOTS = 4
ROWS = HD + 16
BF, F32 = jnp.bfloat16, jnp.float32
LOG2E = 1.4426950408889634
C2 = LOG2E * HD**-0.5
LOW = -1e30
VMEM = 48 * 1024 * 1024
HEAD_GROUPS = ((0,), (1,), (2,), (3,))


def send(block, dy=0, dz=0, dc=0):
    route = []
    for y in range(NY):
        for z in range(NZ):
            for c in range(NC):
                to = (((y + dy) % NY) * NZ + (z + dz) % NZ) * NC + (c + dc) % NC
                route.append(((y * NZ + z) * NC + c, to))
    return lax.ppermute(block, "mem", route)


def send_x(block, dx):
    return lax.ppermute(block, "blk", [(x, (x + dx) % NX) for x in range(NX)])


def nt(a, b):
    return lax.dot_general(a, b, (((1,), (1,)), ((), ())), preferred_element_type=F32)


def cost(flops, bytes_accessed, exps=0):
    return pl.CostEstimate(
        flops=int(flops), bytes_accessed=int(bytes_accessed), transcendentals=int(exps)
    )


def params():
    return pltpu.CompilerParams(vmem_limit_bytes=VMEM)


def pack_kernel(k_ref, v_ref, *outs):
    for h in range(NH):
        cols = slice(h * HD, (h + 1) * HD)
        outs[h][0] = k_ref[:, :, cols]
        for s in range(SLOTS):
            outs[h][1, s] = v_ref[s, :, cols].T


def pack(keys, values):
    shape = jax.ShapeDtypeStruct((2, SLOTS, BT, HD), BF)
    return pl.pallas_call(
        pack_kernel,
        out_shape=[shape] * NH,
        name="pack",
        compiler_params=params(),
        cost_estimate=cost(0, 2**21),
    )(keys, values)


def gate_of(q, row):
    logit = jnp.sum(q.astype(F32) * row, axis=1, keepdims=True) * F32(HD**-0.5)
    return 1.0 / (1.0 + jnp.exp(-logit))


def local_kernel(first_ref, q_ref, kp_ref, ko_ref, vp_ref, vo_ref, g_ref, out_ref, k_all, v_all):
    k_all[:TOK] = kp_ref[...]
    k_all[TOK:] = ko_ref[...]
    v_all[:TOK] = vp_ref[...]
    v_all[TOK:] = vo_ref[...]
    start = first_ref[0]
    span = TOK + BT
    row = lax.broadcasted_iota(jnp.int32, (BT, span), 0)
    col = lax.broadcasted_iota(jnp.int32, (BT, span), 1)
    band = (col > row) & (col <= row + TOK)
    for b in range(QB):
        q = q_ref[b * BT : (b + 1) * BT]
        s = nt(q, k_all[b * BT : b * BT + span])
        s = jnp.where(band & (col + b * BT >= start), s, LOW)
        top = jnp.max(s, axis=1, keepdims=True)
        p = jnp.exp2((s - top) * C2)
        total = jnp.sum(p, axis=1, keepdims=True)
        o = jnp.dot(p.astype(BF), v_all[b * BT : b * BT + span], preferred_element_type=F32)
        gate = gate_of(q, g_ref[0])
        out_ref[b * BT : (b + 1) * BT] = o * ((1.0 - gate) / total)


def local(head, first, q, kp, ko, vp, vo, gate_rows):
    spec = pl.BlockSpec((TOK, HD), lambda i: (0, head))
    return pl.pallas_call(
        local_kernel,
        out_shape=jax.ShapeDtypeStruct((TOK, HD), F32),
        grid=(1,),
        in_specs=[pl.BlockSpec(memory_space=pltpu.SMEM)]
        + [spec] * 5
        + [pl.BlockSpec((1, 1, HD), lambda i: (head, 0, 0))],
        out_specs=pl.BlockSpec((TOK, HD), lambda i: (0, 0)),
        scratch_shapes=[pltpu.VMEM((2 * TOK, HD), BF)] * 2,
        name="local",
        compiler_params=params(),
        cost_estimate=cost(4 * TOK * 640 * HD, 2**20, TOK * 640),
    )(first, q, kp, ko, vp, vo, gate_rows)


def write_part(ref, where, value, lse):
    ref[(*where, pl.ds(0, HD))] = value.astype(BF)
    hi = lse.astype(BF)
    rest = lse - hi.astype(F32)
    mid = rest.astype(BF)
    lo = (rest - mid.astype(F32)).astype(BF)
    n = lax.broadcasted_iota(jnp.int32, (ROWS - HD, BT), 0)
    tail = jnp.where(
        n == 0,
        hi.astype(F32),
        jnp.where(n == 1, mid.astype(F32), jnp.where(n == 2, lo.astype(F32), 0.0)),
    )
    ref[(*where, pl.ds(HD, ROWS - HD))] = tail.astype(BF)


def read_part(ref, where):
    tail = ref[(*where, pl.ds(HD, ROWS - HD))].astype(F32)
    return ref[(*where, pl.ds(0, HD))].astype(F32), jnp.sum(tail, axis=0, keepdims=True)


def mem_kernel(table, *refs):
    qs, kvs, outs, (acc,) = refs[:2], refs[2:10], refs[10:12], refs[12:]

    def one(dy, carry):
        for dc in range(NC):
            entry = [table[dc, dy, o] for o in range(NZ)]
            valid = [e > 0 for e in entry]
            place = [jnp.maximum(e - 1, 0) for e in entry]
            block = [p // SLOTS for p in place]
            slot = [p % SLOTS for p in place]
            scores, tops = [], []
            for o in range(NZ):
                q = qs[dc][dy, pl.ds(pl.multiple_of(block[o] * BT, BT), BT), :]
                s = nt(kvs[o][0, slot[o]], q)
                scores.append(s)
                tops.append(jnp.max(s, axis=0, keepdims=True))
            top = []
            for b in range(QB):
                best = jnp.full((1, BT), LOW, F32)
                for o in range(NZ):
                    best = jnp.maximum(best, jnp.where(valid[o] & (block[o] == b), tops[o], LOW))
                top.append(best)
            acc[...] = jnp.zeros_like(acc)
            total = [jnp.zeros((1, BT), F32) for _ in range(QB)]
            for o in range(NZ):
                mine = jnp.full((1, BT), -LOW, F32)
                for b in range(QB):
                    mine = jnp.where(valid[o] & (block[o] == b), top[b], mine)
                p = jnp.exp2((scores[o] - mine) * C2)
                size = jnp.sum(p, axis=0, keepdims=True)
                for b in range(QB):
                    total[b] += jnp.where(block[o] == b, size, 0.0)
                acc[block[o]] += jnp.dot(
                    kvs[o][1, slot[o]], p.astype(BF), preferred_element_type=F32
                )
            for b in range(QB):
                some = total[b] > 0
                safe = jnp.where(some, total[b], 1.0)
                lse = jnp.where(some, top[b] * C2 + jnp.log2(safe), LOW)
                write_part(outs[dc], (dy, b), acc[b] * (1.0 / safe), lse)
        return carry

    lax.fori_loop(0, NY, one, 0)


def mem_attention(head, table, qa, qb, kvs):
    part = jax.ShapeDtypeStruct((NY, QB, ROWS, BT), BF)
    qspec = pl.BlockSpec((NY, TOK, HD), lambda i: (0, 0, head))
    whole = pl.BlockSpec((2, SLOTS, BT, HD), lambda i: (0, 0, 0, 0))
    out = pl.BlockSpec((NY, QB, ROWS, BT), lambda i: (0, 0, 0, 0))
    return pl.pallas_call(
        mem_kernel,
        out_shape=[part] * NC,
        grid=(1,),
        in_specs=[pl.BlockSpec(memory_space=pltpu.SMEM)] + [qspec] * 2 + [whole] * NZ,
        out_specs=[out] * NC,
        scratch_shapes=[pltpu.VMEM((QB, HD, BT), F32)],
        name="memory",
        compiler_params=params(),
        cost_estimate=cost(64 * 4 * BT * BT * HD, 5 * 2**20, 64 * BT * BT),
    )(table, qa, qb, *kvs)


def merged(parts):
    values = [v for v, _ in parts]
    tops = [t for _, t in parts]
    best = functools.reduce(jnp.maximum, tops)
    weights = [jnp.exp2(t - best) for t in tops]
    total = sum(weights)
    share = 1.0 / total
    return sum(v * (w * share) for v, w in zip(values, weights)), best + jnp.log2(total)


def pair_kernel(a_ref, b_ref, *outs):
    for dy in range(NY):
        for b in range(QB):
            value, lse = merged([read_part(a_ref, (dy, b)), read_part(b_ref, (dy, b))])
            write_part(outs[dy], (b,), value, lse)


def pair(a, b):
    return pl.pallas_call(
        pair_kernel,
        out_shape=[jax.ShapeDtypeStruct((QB, ROWS, BT), BF)] * NY,
        name="pair",
        compiler_params=params(),
        cost_estimate=cost(2**21, 2**21),
    )(a, b)


def finish_kernel(p0, p1, p2, p3, loc_ref, q_ref, g_ref, out_ref):
    for b in range(QB):
        value, _ = merged([read_part(p, (b,)) for p in (p0, p1, p2, p3)])
        rows = slice(b * BT, (b + 1) * BT)
        gate = gate_of(q_ref[rows], g_ref[0])
        out_ref[rows] = (gate * value.T + loc_ref[rows]).astype(BF)


def finish(head, parts, loc, q, gate_rows):
    part = pl.BlockSpec((QB, ROWS, BT), lambda i: (0, 0, 0))
    return pl.pallas_call(
        finish_kernel,
        out_shape=jax.ShapeDtypeStruct((TOK, HD), BF),
        grid=(1,),
        in_specs=[part] * 4
        + [
            pl.BlockSpec((TOK, HD), lambda i: (0, 0)),
            pl.BlockSpec((TOK, HD), lambda i: (0, head)),
            pl.BlockSpec((1, 1, HD), lambda i: (head, 0, 0)),
        ],
        out_specs=pl.BlockSpec((TOK, HD), lambda i: (0, 0)),
        name="finish",
        compiler_params=params(),
        cost_estimate=cost(2**20, 2**20),
    )(*parts, loc, q, gate_rows)


def project_kernel(n, last, source, *refs):
    atts, weights, rest = refs[:n], refs[n : 2 * n], refs[2 * n :]
    total = None
    for a, w in zip(atts, weights):
        term = jnp.dot(a[...], w[...], preferred_element_type=F32)
        total = term if total is None else total + term
    if len(rest) == 2:
        total = total + rest[0][...]
    rest[-1][...] = total.astype(rest[-1].dtype)


def project(source, atts, out_weight, before, last):
    n = len(atts)
    width = out_weight.shape[1]
    tile = 256

    def weight_spec(head, k):
        return pl.BlockSpec((HD, tile), lambda i, src: (src[k] * NH + head, i))

    acc = pl.BlockSpec((TOK, tile), lambda i, src: (0, i))
    in_specs = [pl.BlockSpec((TOK, HD), lambda i, src: (0, 0))] * n
    in_specs += [weight_spec(head, k) for head, k, _ in atts]
    operands = [a for _, _, a in atts] + [out_weight] * n
    if before is not None:
        in_specs.append(acc)
        operands.append(before)
    return pl.pallas_call(
        functools.partial(project_kernel, n, last),
        out_shape=jax.ShapeDtypeStruct((TOK, width), BF if last else F32),
        grid_spec=pltpu.PrefetchScalarGridSpec(
            num_scalar_prefetch=1,
            grid=(width // tile,),
            in_specs=in_specs,
            out_specs=acc,
        ),
        name="project",
        compiler_params=params(),
        cost_estimate=cost(2 * TOK * HD * n * width, 6 * 2**20),
    )(source, *operands)


def shards(
    queries,
    local_keys,
    local_values,
    memory_keys,
    memory_values,
    block_ids,
    gate_index,
    gate_vectors,
    out_weight,
):
    me = lax.axis_index("mem")
    y, z, c = me // (NZ * NC), (me // NC) % NZ, me % NC
    x = lax.axis_index("blk")
    kv = pack(memory_keys, memory_values)

    near = [queries, send(queries, dy=1), send(queries, dy=2), send(queries, dy=3)]
    qa = jnp.stack(near)
    qb = send(qa, dc=1)
    every = lax.all_gather(block_ids.reshape(-1), "mem").reshape(NY, NZ, NC, -1)
    plane = lax.dynamic_index_in_dim(every, z, 1, keepdims=False)
    back = (y - jnp.arange(NY, dtype=jnp.int32)) % NY
    sides = (c + jnp.arange(NC, dtype=jnp.int32)) % NC
    ids = plane[back[None, :], sides[:, None]]
    owners = (y * NZ + (z - jnp.arange(NZ, dtype=jnp.int32)) % NZ) * NC + c
    position = jnp.arange(ids.shape[-1], dtype=jnp.int32) // block_ids.shape[1]
    code = 1 + position * SLOTS + ids % SLOTS
    hit = (ids // SLOTS)[:, :, None, :] == owners[None, None, :, None]
    table = jnp.sum(jnp.where(hit, code[:, :, None, :], 0), axis=-1)

    route = [(i, i + 1) for i in range(NY * NZ * NC - 1)]
    kp = lax.ppermute(local_keys, "mem", route)
    vp = lax.ppermute(local_values, "mem", route)
    first = jnp.where(me > 0, 0, TOK).astype(jnp.int32)[None]
    which = gate_index[:, None] == jnp.arange(gate_vectors.shape[0], dtype=jnp.int32)[None, :]
    gate_rows = jnp.sum(jnp.where(which[:, :, None], gate_vectors[None], 0.0), axis=1)[:, None, :]

    source = ((x - jnp.arange(NX, dtype=jnp.int32)) % NX).astype(jnp.int32)
    gathered = []
    before = None
    gone = None
    for h in range(NH):
        own = kv[h]
        if gone is not None:
            own, _ = lax.optimization_barrier((own, gone))
        ups, downs = (4, 3) if h == NH - 1 else (3, 4)
        up, down = [own], [own]
        for _ in range(ups):
            up.append(send(up[-1], dz=1))
        for _ in range(downs):
            down.append(send(down[-1], dz=-1))
        gone = (up[2], down[2])
        kvs = up + down[:0:-1]
        loc = local(h, first, queries, kp, local_keys, vp, local_values, gate_rows)
        pa, pb = mem_attention(h, table, qa, qb, kvs)
        m = pair(pa, send(pb, dc=1))
        parts = [m[0], send(m[1], dy=-1), send(m[2], dy=-2), send(m[3], dy=-3)]
        att = finish(h, parts, loc, queries, gate_rows)
        gathered += [(h, k, att if k == 0 else send_x(att, k)) for k in range(NX)]
        if h == NH - 2:
            before = project(source, gathered, out_weight, None, False)
            gathered = []
    return project(source, gathered, out_weight, before, True)


def solution(mesh):
    placed = (
        P("mem", "blk"),
        P("mem", "blk"),
        P("mem", "blk"),
        P("mem", None, "blk"),
        P("mem", None, "blk"),
        P("mem", None),
        P("blk"),
        P(),
        P(None, "blk"),
    )
    return jax.shard_map(
        shards, mesh=mesh, in_specs=placed, out_specs=P("mem", "blk"), check_vma=False
    )
```

```python
import functools

import jax
import jax.numpy as jnp
from jax import lax
from jax.experimental import pallas as pl
from jax.experimental.pallas import tpu as pltpu
from jax.sharding import PartitionSpec as P

NY, NZ, NC, NX = 4, 8, 2, 4
HD = 128
BT = 128
TOK = 512
NH = 4
QB = 4
SLOTS = 4
EXTRA = 16
ROWS = HD + EXTRA
BF, F32 = jnp.bfloat16, jnp.float32
LOG2E = 1.4426950408889634
C2 = LOG2E * HD**-0.5
LOW = -1e30
MIB = 1024 * 1024
GROUPS = ((0, 2), (2, 2))


def send(block, dy=0, dz=0, dc=0):
    route = []
    for y in range(NY):
        for z in range(NZ):
            for c in range(NC):
                to = (((y + dy) % NY) * NZ + (z + dz) % NZ) * NC + (c + dc) % NC
                route.append(((y * NZ + z) * NC + c, to))
    return lax.ppermute(block, "mem", route)


def send_x(block, dx):
    return lax.ppermute(block, "blk", [(x, (x + dx) % NX) for x in range(NX)])


def nt(a, b):
    return lax.dot_general(a, b, (((1,), (1,)), ((), ())), preferred_element_type=F32)


def cost(flops, bytes_accessed, exps=0):
    return pl.CostEstimate(
        flops=int(flops), bytes_accessed=int(bytes_accessed), transcendentals=int(exps)
    )


def params(size=16):
    return pltpu.CompilerParams(vmem_limit_bytes=size * MIB)


def pack_kernel(k_ref, v_ref, *outs):
    for out, (head, n) in zip(outs, GROUPS):
        for i in range(n):
            cols = slice((head + i) * HD, (head + i + 1) * HD)
            for s in range(SLOTS):
                out[0, i, s] = k_ref[s, :, cols]
                out[1, i, s] = v_ref[s, :, cols].T


def pack(keys, values):
    return pl.pallas_call(
        pack_kernel,
        out_shape=[jax.ShapeDtypeStruct((2, n, SLOTS, BT, HD), BF) for _, n in GROUPS],
        name="pack",
        compiler_params=params(),
        cost_estimate=cost(0, 2**21),
    )(keys, values)


def gate_of(q, row):
    logit = jnp.sum(q.astype(F32) * row, axis=1, keepdims=True) * F32(HD**-0.5)
    return 1.0 / (1.0 + jnp.exp(-logit))


def local_kernel(first_ref, q_ref, kp_ref, ko_ref, vp_ref, vo_ref, g_ref, out_ref, k_all, v_all):
    k_all[:TOK] = kp_ref[...]
    k_all[TOK:] = ko_ref[...]
    v_all[:TOK] = vp_ref[...]
    v_all[TOK:] = vo_ref[...]
    start = first_ref[0]
    span = TOK + BT
    row = lax.broadcasted_iota(jnp.int32, (BT, span), 0)
    col = lax.broadcasted_iota(jnp.int32, (BT, span), 1)
    band = (col > row) & (col <= row + TOK)
    for b in range(QB):
        q = q_ref[b * BT : (b + 1) * BT]
        s = nt(q, k_all[b * BT : b * BT + span])
        s = jnp.where(band & (col + b * BT >= start), s, LOW)
        top = jnp.max(s, axis=1, keepdims=True)
        p = jnp.exp2((s - top) * C2)
        total = jnp.sum(p, axis=1, keepdims=True)
        o = jnp.dot(p.astype(BF), v_all[b * BT : b * BT + span], preferred_element_type=F32)
        gate = gate_of(q, g_ref[0])
        out_ref[b * BT : (b + 1) * BT] = o * ((1.0 - gate) / total)


def local(group, first, q, kp, ko, vp, vo, gate_rows):
    head, n = group
    spec = pl.BlockSpec((TOK, HD), lambda i: (0, head + i))
    return pl.pallas_call(
        local_kernel,
        out_shape=jax.ShapeDtypeStruct((TOK, n * HD), F32),
        grid=(n,),
        in_specs=[pl.BlockSpec(memory_space=pltpu.SMEM)]
        + [spec] * 5
        + [pl.BlockSpec((1, 1, HD), lambda i: (head + i, 0, 0))],
        out_specs=pl.BlockSpec((TOK, HD), lambda i: (0, i)),
        scratch_shapes=[pltpu.VMEM((2 * TOK, HD), BF)] * 2,
        name="local",
        compiler_params=params(),
        cost_estimate=cost(n * 4 * TOK * 640 * HD, n * 2**20, n * TOK * 640),
    )(first, q, kp, ko, vp, vo, gate_rows)


def write_part(ref, where, value, lse):
    ref[(*where, pl.ds(0, HD))] = value.astype(BF)
    hi = lse.astype(BF)
    rest = lse - hi.astype(F32)
    mid = rest.astype(BF)
    lo = (rest - mid.astype(F32)).astype(BF)
    n = lax.broadcasted_iota(jnp.int32, (EXTRA, BT), 0)
    tail = jnp.where(
        n == 0,
        hi.astype(F32),
        jnp.where(n == 1, mid.astype(F32), jnp.where(n == 2, lo.astype(F32), 0.0)),
    )
    ref[(*where, pl.ds(HD, EXTRA))] = tail.astype(BF)


def read_part(ref, where):
    tail = ref[(*where, pl.ds(HD, EXTRA))].astype(F32)
    return ref[(*where, pl.ds(0, HD))].astype(F32), jnp.sum(tail, axis=0, keepdims=True)


def mem_kernel(n, table, *refs):
    qs, ks, vs, outs, accs = refs[:2], refs[2:18:2], refs[3:18:2], refs[18:20], refs[20]

    def one(dy, carry):
        for dc in range(NC):
            entry = [table[dc, dy, o] for o in range(NZ)]
            valid = [e > 0 for e in entry]
            place = [jnp.maximum(e - 1, 0) for e in entry]
            block = [p // SLOTS for p in place]
            slot = [p % SLOTS for p in place]
            for i in range(n):
                acc = accs.at[dc * n + i]
                scores, tops = [], []
                for o in range(NZ):
                    q = qs[dc][
                        dy, pl.ds(pl.multiple_of(block[o] * BT, BT), BT), i * HD : (i + 1) * HD
                    ]
                    s = nt(ks[o][0, i, slot[o]], q)
                    scores.append(s)
                    tops.append(jnp.max(s, axis=0, keepdims=True))
                top = []
                for b in range(QB):
                    best = jnp.full((1, BT), LOW, F32)
                    for o in range(NZ):
                        here = valid[o] & (block[o] == b)
                        best = jnp.maximum(best, jnp.where(here, tops[o], LOW))
                    top.append(best)
                acc[...] = jnp.zeros_like(acc)
                total = [jnp.zeros((1, BT), F32) for _ in range(QB)]
                for o in range(NZ):
                    mine = jnp.full((1, BT), -LOW, F32)
                    for b in range(QB):
                        mine = jnp.where(valid[o] & (block[o] == b), top[b], mine)
                    p = jnp.exp2((scores[o] - mine) * C2)
                    size = jnp.sum(p, axis=0, keepdims=True)
                    for b in range(QB):
                        total[b] += jnp.where(block[o] == b, size, 0.0)
                    acc[block[o]] += jnp.dot(
                        vs[o][0, i, slot[o]], p.astype(BF), preferred_element_type=F32
                    )
                for b in range(QB):
                    some = total[b] > 0
                    safe = jnp.where(some, total[b], 1.0)
                    lse = jnp.where(some, top[b] * C2 + jnp.log2(safe), LOW)
                    write_part(outs[dc], (dy, i, b), acc[b] * (1.0 / safe), lse)
        return carry

    lax.fori_loop(0, NY, one, 0)


def mem_attention(group, table, qa, qb, kvs):
    head, n = group
    part = jax.ShapeDtypeStruct((NY, n, QB, ROWS, BT), BF)
    qspec = pl.BlockSpec((NY, TOK, n * HD), lambda i: (0, 0, head // n))
    operands, specs = [], []
    for array, index in kvs:
        operands.append(array)
        specs.append(
            pl.BlockSpec((1, n, SLOTS, BT, HD), lambda i, index=index: (index, 0, 0, 0, 0))
        )
    out = pl.BlockSpec((NY, n, QB, ROWS, BT), lambda i: (0, 0, 0, 0, 0))
    return pl.pallas_call(
        functools.partial(mem_kernel, n),
        out_shape=[part] * NC,
        grid=(1,),
        in_specs=[pl.BlockSpec(memory_space=pltpu.SMEM)] + [qspec] * 2 + specs,
        out_specs=[out] * NC,
        scratch_shapes=[pltpu.VMEM((NC * n, QB, HD, BT), F32)],
        name="memory",
        compiler_params=params(26),
        cost_estimate=cost(n * 64 * 4 * BT * BT * HD, n * 5 * 2**20, n * 64 * BT * BT),
    )(table, qa, qb, *operands)


def merged(parts):
    values = [v for v, _ in parts]
    tops = [t for _, t in parts]
    best = functools.reduce(jnp.maximum, tops)
    weights = [jnp.exp2(t - best) for t in tops]
    total = sum(weights)
    share = 1.0 / total
    return sum(v * (w * share) for v, w in zip(values, weights)), best + jnp.log2(total)


def pair_kernel(n, a_ref, *refs):
    others, outs = refs[: NY * n], refs[NY * n :]
    for dy in range(NY):
        for i in range(n):
            for b in range(QB):
                both = [read_part(a_ref, (dy, i, b)), read_part(others[dy * n + i], (b,))]
                value, lse = merged(both)
                write_part(outs[dy], (i, b), value, lse)


def pair(group, a, b):
    n = group[1]
    others = [send(b[dy, i], dc=1) for dy in range(NY) for i in range(n)]
    return pl.pallas_call(
        functools.partial(pair_kernel, n),
        out_shape=[jax.ShapeDtypeStruct((n, QB, ROWS, BT), BF)] * NY,
        name="pair",
        compiler_params=params(),
        cost_estimate=cost(n * 2**21, n * 2**21),
    )(a, *others)


def finish_kernel(p0, p1, p2, p3, loc_ref, q_ref, g_ref, out_ref):
    for b in range(QB):
        value, _ = merged([read_part(p, (0, b)) for p in (p0, p1, p2, p3)])
        rows = slice(b * BT, (b + 1) * BT)
        gate = gate_of(q_ref[rows], g_ref[0])
        out_ref[rows] = (gate * value.T + loc_ref[rows]).astype(BF)


def finish(group, parts, loc, q, gate_rows):
    head, n = group
    part = pl.BlockSpec((1, QB, ROWS, BT), lambda i: (i, 0, 0, 0))
    return pl.pallas_call(
        finish_kernel,
        out_shape=jax.ShapeDtypeStruct((TOK, n * HD), BF),
        grid=(n,),
        in_specs=[part] * 4
        + [
            pl.BlockSpec((TOK, HD), lambda i: (0, i)),
            pl.BlockSpec((TOK, HD), lambda i: (0, head + i)),
            pl.BlockSpec((1, 1, HD), lambda i: (head + i, 0, 0)),
        ],
        out_specs=pl.BlockSpec((TOK, HD), lambda i: (0, i)),
        name="finish",
        compiler_params=params(),
        cost_estimate=cost(n * 2**20, n * 2**20),
    )(*parts, loc, q, gate_rows)


def project_kernel(n, source, *refs):
    atts, weights, rest = refs[:n], refs[n : 2 * n], refs[2 * n :]
    total = rest[0][...] if len(rest) == 2 else None
    for a, w in zip(atts, weights):
        term = jnp.dot(a[...], w[...], preferred_element_type=F32)
        total = term if total is None else total + term
    rest[-1][...] = total.astype(rest[-1].dtype)


def project(source, pieces, out_weight, before, last):
    m = len(pieces)
    width = out_weight.shape[1]
    tile = 512

    def weight_spec(group, k):
        head, n = group
        return pl.BlockSpec((n * HD, tile), lambda i, src: ((src[k] * NH + head) // n, i))

    acc = pl.BlockSpec((TOK, tile), lambda i, src: (0, i))
    in_specs = [pl.BlockSpec((TOK, g[1] * HD), lambda i, src: (0, 0)) for g, _, _ in pieces]
    in_specs += [weight_spec(g, k) for g, k, _ in pieces]
    operands = [a for _, _, a in pieces] + [out_weight] * m
    if before is not None:
        in_specs.append(acc)
        operands.append(before)
    depth = sum(g[1] for g, _, _ in pieces) * HD
    return pl.pallas_call(
        functools.partial(project_kernel, m),
        out_shape=jax.ShapeDtypeStruct((TOK, width), BF if last else F32),
        grid_spec=pltpu.PrefetchScalarGridSpec(
            num_scalar_prefetch=1,
            grid=(width // tile,),
            in_specs=in_specs,
            out_specs=acc,
        ),
        name="project",
        compiler_params=params(),
        cost_estimate=cost(2 * TOK * depth * width, 6 * 2**20),
    )(source, *operands)


def after(block, *others):
    return lax.optimization_barrier((block, *others))[0]


def step(chain, dz, *others):
    chain.append(send(after(chain[-1], *others) if others else chain[-1], dz=dz))


def shards(
    queries,
    local_keys,
    local_values,
    memory_keys,
    memory_values,
    block_ids,
    gate_index,
    gate_vectors,
    out_weight,
):
    me = lax.axis_index("mem")
    y, z, c = me // (NZ * NC), (me // NC) % NZ, me % NC
    x = lax.axis_index("blk")
    kv = pack(memory_keys, memory_values)

    wanted = block_ids.size
    note = jnp.pad(block_ids.reshape(1, -1).astype(BF), ((0, EXTRA - 1), (0, NH * HD - wanted)))
    ga, gb = GROUPS
    up_a, down_a = [kv[0]], [kv[0]]
    step(up_a, 1)
    step(down_a, -1)
    noted = after(jnp.concatenate([queries, note]), up_a[1])
    near = [noted, send(noted, dy=1), send(noted, dy=2), send(noted, dy=3)]
    qa = jnp.stack(near)
    qb = jnp.stack([send(q, dc=1) for q in near])
    ids = jnp.stack([qa[:, TOK, :wanted], qb[:, TOK, :wanted]]).astype(jnp.int32)
    owners = (y * NZ + (z - jnp.arange(NZ, dtype=jnp.int32)) % NZ) * NC + c
    position = jnp.arange(wanted, dtype=jnp.int32) // block_ids.shape[1]
    code = 1 + position * SLOTS + ids % SLOTS
    hit = (ids // SLOTS)[:, :, None, :] == owners[None, None, :, None]
    table = jnp.sum(jnp.where(hit, code[:, :, None, :], 0), axis=-1)

    route = [(i, i + 1) for i in range(NY * NZ * NC - 1)]
    kp = lax.ppermute(local_keys, "mem", route)
    vp = lax.ppermute(local_values, "mem", route)
    first = jnp.where(me > 0, 0, TOK).astype(jnp.int32)[None]
    which = gate_index[:, None] == jnp.arange(gate_vectors.shape[0], dtype=jnp.int32)[None, :]
    gate_rows = jnp.sum(jnp.where(which[:, :, None], gate_vectors[None], 0.0), axis=1)[:, None, :]
    source = ((x - jnp.arange(NX, dtype=jnp.int32)) % NX).astype(jnp.int32)
    step(up_a, 1)
    step(down_a, -1)
    up_b, down_b = [after(kv[1], up_a[2])], [after(kv[1], down_a[2])]
    loc_a = local(ga, first, queries, kp, local_keys, vp, local_values, gate_rows)
    step(up_a, 1)
    step(down_a, -1)
    step(up_b, 1)
    step(down_b, -1)
    loc_b = local(gb, first, queries, kp, local_keys, vp, local_values, gate_rows)
    step(down_a, -1, loc_a)
    step(up_b, 1, loc_b)
    step(down_b, -1, loc_b)
    step(up_b, 1)
    step(down_b, -1)
    kvs = [(a, j) for a in up_a + down_a[:0:-1] for j in range(2)]
    pa, pb = mem_attention(ga, table, qa, qb, kvs)
    far = [(send(after(up_b[3], pa)[:1], dz=1), 0), (send(after(down_b[3], pa)[1:], dz=-1), 0)]
    m = pair(ga, pa, pb)
    parts = [m[0], send(m[1], dy=-1), send(m[2], dy=-2), send(m[3], dy=-3)]
    att_a = finish(ga, parts, loc_a, queries, gate_rows)
    pieces = [(ga, k, att_a if k == 0 else send_x(att_a, k)) for k in range(NX)]
    before = project(source, pieces, out_weight, None, False)

    kvs = [(a, j) for a in up_b for j in range(2)] + far
    kvs += [(a, j) for a in down_b[:0:-1] for j in range(2)]
    pa, pb = mem_attention(gb, after(table, m[0]), qa, qb, kvs)
    m = pair(gb, after(pa, att_a), pb)
    parts = [m[0], send(m[1], dy=-1), send(m[2], dy=-2), send(m[3], dy=-3)]
    att = finish(gb, parts, after(loc_b, before), queries, gate_rows)
    pieces = [(gb, k, att if k == 0 else send_x(att, k)) for k in range(NX)]
    return project(source, pieces, out_weight, before, True)


def solution(mesh):
    placed = (
        P("mem", "blk"),
        P("mem", "blk"),
        P("mem", "blk"),
        P("mem", None, "blk"),
        P("mem", None, "blk"),
        P("mem", None),
        P("blk"),
        P(),
        P(None, "blk"),
    )
    return jax.shard_map(
        shards, mesh=mesh, in_specs=placed, out_specs=P("mem", "blk"), check_vma=False
    )
```

```python
import functools

import jax
import jax.numpy as jnp
from jax import lax
from jax.experimental import pallas as pl
from jax.experimental.pallas import tpu as pltpu
from jax.sharding import PartitionSpec as P

NY, NZ, NC, NX = 4, 8, 2, 4
HD = 128
BT = 128
TOK = 512
NH = 4
QB = 4
SLOTS = 4
EXTRA = 16
ROWS = HD + EXTRA
BF, F32 = jnp.bfloat16, jnp.float32
LOG2E = 1.4426950408889634
C2 = LOG2E * HD**-0.5
LOW = -1e30
MIB = 1024 * 1024
GROUPS = ((0, 2), (2, 2))


def send(block, dy=0, dz=0, dc=0):
    route = []
    for y in range(NY):
        for z in range(NZ):
            for c in range(NC):
                to = (((y + dy) % NY) * NZ + (z + dz) % NZ) * NC + (c + dc) % NC
                route.append(((y * NZ + z) * NC + c, to))
    return lax.ppermute(block, "mem", route)


def send_x(block, dx):
    return lax.ppermute(block, "blk", [(x, (x + dx) % NX) for x in range(NX)])


def nt(a, b):
    return lax.dot_general(a, b, (((1,), (1,)), ((), ())), preferred_element_type=F32)


def cost(flops, bytes_accessed, exps=0):
    return pl.CostEstimate(
        flops=int(flops), bytes_accessed=int(bytes_accessed), transcendentals=int(exps)
    )


def params(size=16):
    return pltpu.CompilerParams(vmem_limit_bytes=size * MIB)


def pack_kernel(k_ref, v_ref, *outs):
    for out, (head, n) in zip(outs, GROUPS):
        for i in range(n):
            cols = slice((head + i) * HD, (head + i + 1) * HD)
            for s in range(SLOTS):
                out[0, i, s] = k_ref[s, :, cols]
                out[1, i, s] = v_ref[s, :, cols].T


def pack(keys, values):
    return pl.pallas_call(
        pack_kernel,
        out_shape=[jax.ShapeDtypeStruct((2, n, SLOTS, BT, HD), BF) for _, n in GROUPS],
        name="pack",
        compiler_params=params(),
        cost_estimate=cost(0, 2**21),
    )(keys, values)


def gate_of(q, row):
    logit = jnp.sum(q.astype(F32) * row, axis=1, keepdims=True) * F32(HD**-0.5)
    return 1.0 / (1.0 + jnp.exp(-logit))


def local_kernel(first_ref, q_ref, kp_ref, ko_ref, vp_ref, vo_ref, g_ref, out_ref, k_all, v_all):
    k_all[:TOK] = kp_ref[...]
    k_all[TOK:] = ko_ref[...]
    v_all[:TOK] = vp_ref[...]
    v_all[TOK:] = vo_ref[...]
    start = first_ref[0]
    span = TOK + BT
    row = lax.broadcasted_iota(jnp.int32, (BT, span), 0)
    col = lax.broadcasted_iota(jnp.int32, (BT, span), 1)
    band = (col > row) & (col <= row + TOK)
    for b in range(QB):
        q = q_ref[b * BT : (b + 1) * BT]
        s = nt(q, k_all[b * BT : b * BT + span])
        s = jnp.where(band & (col + b * BT >= start), s, LOW)
        top = jnp.max(s, axis=1, keepdims=True)
        p = jnp.exp2((s - top) * C2)
        total = jnp.sum(p, axis=1, keepdims=True)
        o = jnp.dot(p.astype(BF), v_all[b * BT : b * BT + span], preferred_element_type=F32)
        gate = gate_of(q, g_ref[0])
        out_ref[b * BT : (b + 1) * BT] = o * ((1.0 - gate) / total)


def local(group, first, q, kp, ko, vp, vo, gate_rows):
    head, n = group
    spec = pl.BlockSpec((TOK, HD), lambda i: (0, head + i))
    return pl.pallas_call(
        local_kernel,
        out_shape=jax.ShapeDtypeStruct((TOK, n * HD), F32),
        grid=(n,),
        in_specs=[pl.BlockSpec(memory_space=pltpu.SMEM)]
        + [spec] * 5
        + [pl.BlockSpec((1, 1, HD), lambda i: (head + i, 0, 0))],
        out_specs=pl.BlockSpec((TOK, HD), lambda i: (0, i)),
        scratch_shapes=[pltpu.VMEM((2 * TOK, HD), BF)] * 2,
        name="local",
        compiler_params=params(),
        cost_estimate=cost(n * 4 * TOK * 640 * HD, n * 2**20, n * TOK * 640),
    )(first, q, kp, ko, vp, vo, gate_rows)


def write_part(ref, where, value, lse):
    ref[(*where, pl.ds(0, HD))] = value.astype(BF)
    hi = lse.astype(BF)
    rest = lse - hi.astype(F32)
    mid = rest.astype(BF)
    lo = (rest - mid.astype(F32)).astype(BF)
    n = lax.broadcasted_iota(jnp.int32, (EXTRA, BT), 0)
    tail = jnp.where(
        n == 0,
        hi.astype(F32),
        jnp.where(n == 1, mid.astype(F32), jnp.where(n == 2, lo.astype(F32), 0.0)),
    )
    ref[(*where, pl.ds(HD, EXTRA))] = tail.astype(BF)


def read_part(ref, where):
    tail = ref[(*where, pl.ds(HD, EXTRA))].astype(F32)
    return ref[(*where, pl.ds(0, HD))].astype(F32), jnp.sum(tail, axis=0, keepdims=True)


def mem_kernel(n, table, *refs):
    qs, ks, vs, outs, accs = refs[:2], refs[2:18:2], refs[3:18:2], refs[18:20], refs[20]

    def one(dy, carry):
        for dc in range(NC):
            entry = [table[dc, dy, o] for o in range(NZ)]
            valid = [e > 0 for e in entry]
            place = [jnp.maximum(e - 1, 0) for e in entry]
            block = [p // SLOTS for p in place]
            slot = [p % SLOTS for p in place]
            for i in range(n):
                acc = accs.at[dc * n + i]
                scores, tops = [], []
                for o in range(NZ):
                    q = qs[dc][
                        dy, pl.ds(pl.multiple_of(block[o] * BT, BT), BT), i * HD : (i + 1) * HD
                    ]
                    s = nt(ks[o][0, i, slot[o]], q)
                    scores.append(s)
                    tops.append(jnp.max(s, axis=0, keepdims=True))
                top = []
                for b in range(QB):
                    best = jnp.full((1, BT), LOW, F32)
                    for o in range(NZ):
                        here = valid[o] & (block[o] == b)
                        best = jnp.maximum(best, jnp.where(here, tops[o], LOW))
                    top.append(best)
                acc[...] = jnp.zeros_like(acc)
                total = [jnp.zeros((1, BT), F32) for _ in range(QB)]
                for o in range(NZ):
                    mine = jnp.full((1, BT), -LOW, F32)
                    for b in range(QB):
                        mine = jnp.where(valid[o] & (block[o] == b), top[b], mine)
                    p = jnp.exp2((scores[o] - mine) * C2)
                    size = jnp.sum(p, axis=0, keepdims=True)
                    for b in range(QB):
                        total[b] += jnp.where(block[o] == b, size, 0.0)
                    acc[block[o]] += jnp.dot(
                        vs[o][0, i, slot[o]], p.astype(BF), preferred_element_type=F32
                    )
                for b in range(QB):
                    some = total[b] > 0
                    safe = jnp.where(some, total[b], 1.0)
                    lse = jnp.where(some, top[b] * C2 + jnp.log2(safe), LOW)
                    write_part(outs[dc], (dy, i, b), acc[b] * (1.0 / safe), lse)
        return carry

    lax.fori_loop(0, NY, one, 0)


def mem_attention(group, table, qa, qb, kvs):
    head, n = group
    part = jax.ShapeDtypeStruct((NY, n, QB, ROWS, BT), BF)
    qspec = pl.BlockSpec((NY, TOK, n * HD), lambda i: (0, 0, head // n))
    operands, specs = [], []
    for array, index in kvs:
        operands.append(array)
        specs.append(
            pl.BlockSpec((1, n, SLOTS, BT, HD), lambda i, index=index: (index, 0, 0, 0, 0))
        )
    out = pl.BlockSpec((NY, n, QB, ROWS, BT), lambda i: (0, 0, 0, 0, 0))
    return pl.pallas_call(
        functools.partial(mem_kernel, n),
        out_shape=[part] * NC,
        grid=(1,),
        in_specs=[pl.BlockSpec(memory_space=pltpu.SMEM)] + [qspec] * 2 + specs,
        out_specs=[out] * NC,
        scratch_shapes=[pltpu.VMEM((NC * n, QB, HD, BT), F32)],
        name="memory",
        compiler_params=params(26),
        cost_estimate=cost(n * 64 * 4 * BT * BT * HD, n * 5 * 2**20, n * 64 * BT * BT),
    )(table, qa, qb, *operands)


def merged(parts):
    values = [v for v, _ in parts]
    tops = [t for _, t in parts]
    best = functools.reduce(jnp.maximum, tops)
    weights = [jnp.exp2(t - best) for t in tops]
    total = sum(weights)
    share = 1.0 / total
    return sum(v * (w * share) for v, w in zip(values, weights)), best + jnp.log2(total)


def pair_kernel(n, a_ref, *refs):
    others, outs = refs[: NY * n], refs[NY * n :]
    for dy in range(NY):
        for i in range(n):
            for b in range(QB):
                both = [read_part(a_ref, (dy, i, b)), read_part(others[dy * n + i], (b,))]
                value, lse = merged(both)
                write_part(outs[dy], (i, b), value, lse)


def pair(group, a, b):
    n = group[1]
    others = [send(b[dy, i], dc=1) for dy in range(NY) for i in range(n)]
    return pl.pallas_call(
        functools.partial(pair_kernel, n),
        out_shape=[jax.ShapeDtypeStruct((n, QB, ROWS, BT), BF)] * NY,
        name="pair",
        compiler_params=params(),
        cost_estimate=cost(n * 2**21, n * 2**21),
    )(a, *others)


def finish_kernel(p0, p1, p2, p3, loc_ref, q_ref, g_ref, out_ref):
    for b in range(QB):
        value, _ = merged([read_part(p, (0, b)) for p in (p0, p1, p2, p3)])
        rows = slice(b * BT, (b + 1) * BT)
        gate = gate_of(q_ref[rows], g_ref[0])
        out_ref[rows] = (gate * value.T + loc_ref[rows]).astype(BF)


def finish(group, parts, loc, q, gate_rows):
    head, n = group
    part = pl.BlockSpec((1, QB, ROWS, BT), lambda i: (i, 0, 0, 0))
    return pl.pallas_call(
        finish_kernel,
        out_shape=jax.ShapeDtypeStruct((TOK, n * HD), BF),
        grid=(n,),
        in_specs=[part] * 4
        + [
            pl.BlockSpec((TOK, HD), lambda i: (0, i)),
            pl.BlockSpec((TOK, HD), lambda i: (0, head + i)),
            pl.BlockSpec((1, 1, HD), lambda i: (head + i, 0, 0)),
        ],
        out_specs=pl.BlockSpec((TOK, HD), lambda i: (0, i)),
        name="finish",
        compiler_params=params(),
        cost_estimate=cost(n * 2**20, n * 2**20),
    )(*parts, loc, q, gate_rows)


def project_kernel(n, source, *refs):
    atts, weights, rest = refs[:n], refs[n : 2 * n], refs[2 * n :]
    total = rest[0][...] if len(rest) == 2 else None
    for a, w in zip(atts, weights):
        term = jnp.dot(a[...], w[...], preferred_element_type=F32)
        total = term if total is None else total + term
    rest[-1][...] = total.astype(rest[-1].dtype)


def project(source, pieces, out_weight, before, last):
    m = len(pieces)
    width = out_weight.shape[1]
    tile = 512

    def weight_spec(group, k):
        head, n = group
        return pl.BlockSpec((n * HD, tile), lambda i, src: ((src[k] * NH + head) // n, i))

    acc = pl.BlockSpec((TOK, tile), lambda i, src: (0, i))
    in_specs = [pl.BlockSpec((TOK, g[1] * HD), lambda i, src: (0, 0)) for g, _, _ in pieces]
    in_specs += [weight_spec(g, k) for g, k, _ in pieces]
    operands = [a for _, _, a in pieces] + [out_weight] * m
    if before is not None:
        in_specs.append(acc)
        operands.append(before)
    depth = sum(g[1] for g, _, _ in pieces) * HD
    return pl.pallas_call(
        functools.partial(project_kernel, m),
        out_shape=jax.ShapeDtypeStruct((TOK, width), BF if last else F32),
        grid_spec=pltpu.PrefetchScalarGridSpec(
            num_scalar_prefetch=1,
            grid=(width // tile,),
            in_specs=in_specs,
            out_specs=acc,
        ),
        name="project",
        compiler_params=params(),
        cost_estimate=cost(2 * TOK * depth * width, 6 * 2**20),
    )(source, *operands)


def after(block, *others):
    return lax.optimization_barrier((block, *others))[0]


def step(chain, dz, *others):
    chain.append(send(after(chain[-1], *others) if others else chain[-1], dz=dz))


def shards(
    queries,
    local_keys,
    local_values,
    memory_keys,
    memory_values,
    block_ids,
    gate_index,
    gate_vectors,
    out_weight,
):
    me = lax.axis_index("mem")
    y, z, c = me // (NZ * NC), (me // NC) % NZ, me % NC
    x = lax.axis_index("blk")
    kv = pack(memory_keys, memory_values)

    wanted = block_ids.size
    note = jnp.pad(block_ids.reshape(1, -1).astype(BF), ((0, EXTRA - 1), (0, NH * HD - wanted)))
    ga, gb = GROUPS
    up_a, down_a = [kv[0]], [kv[0]]
    step(up_a, 1)
    step(down_a, -1)
    noted = after(jnp.concatenate([queries, note]), up_a[1])
    near = [noted, send(noted, dy=1), send(noted, dy=2), send(noted, dy=3)]
    route = [(i, i + 1) for i in range(NY * NZ * NC - 1)]
    kp = lax.ppermute(local_keys, "mem", route)
    vp = lax.ppermute(local_values, "mem", route)
    first = jnp.where(me > 0, 0, TOK).astype(jnp.int32)[None]
    which = gate_index[:, None] == jnp.arange(gate_vectors.shape[0], dtype=jnp.int32)[None, :]
    gate_rows = jnp.sum(jnp.where(which[:, :, None], gate_vectors[None], 0.0), axis=1)[:, None, :]
    source = ((x - jnp.arange(NX, dtype=jnp.int32)) % NX).astype(jnp.int32)
    step(up_a, 1)
    step(down_a, -1)
    loc_a = local(ga, first, queries, kp, local_keys, vp, local_values, gate_rows)
    loc_b = local(gb, first, queries, kp, local_keys, vp, local_values, gate_rows)
    up_b, down_b = [after(kv[1], up_a[2], loc_a)], [after(kv[1], down_a[2], loc_a)]
    step(up_a, 1)
    step(down_a, -1)
    step(up_b, 1)
    step(down_b, -1)
    near = [after(q, up_b[1], down_b[1]) for q in near]
    qa = jnp.stack(near)
    qb = jnp.stack([send(q, dc=1) for q in near])
    ids = jnp.stack([qa[:, TOK, :wanted], qb[:, TOK, :wanted]]).astype(jnp.int32)
    owners = (y * NZ + (z - jnp.arange(NZ, dtype=jnp.int32)) % NZ) * NC + c
    position = jnp.arange(wanted, dtype=jnp.int32) // block_ids.shape[1]
    code = 1 + position * SLOTS + ids % SLOTS
    hit = (ids // SLOTS)[:, :, None, :] == owners[None, None, :, None]
    table = jnp.sum(jnp.where(hit, code[:, :, None, :], 0), axis=-1)

    step(down_a, -1, loc_b)
    step(up_b, 1)
    step(down_b, -1)
    step(up_b, 1)
    step(down_b, -1)
    kvs = [(a, j) for a in up_a + down_a[:0:-1] for j in range(2)]
    pa, pb = mem_attention(ga, table, qa, qb, kvs)
    far = [(send(after(up_b[3], pa)[:1], dz=1), 0), (send(after(down_b[3], pa)[1:], dz=-1), 0)]
    m = pair(ga, pa, pb)
    parts = [m[0], send(m[1], dy=-1), send(m[2], dy=-2), send(m[3], dy=-3)]
    att_a = finish(ga, parts, loc_a, queries, gate_rows)
    pieces = [(ga, k, att_a if k == 0 else send_x(att_a, k)) for k in range(NX)]
    before = project(source, pieces, out_weight, None, False)

    kvs = [(a, j) for a in up_b for j in range(2)] + far
    kvs += [(a, j) for a in down_b[:0:-1] for j in range(2)]
    pa, pb = mem_attention(gb, after(table, m[0]), qa, qb, kvs)
    m = pair(gb, after(pa, att_a), pb)
    pieces, gone = [], ()
    for i in range(gb[1]):
        one = (gb[0] + i, 1)
        mine = [a[i : i + 1] for a in m]
        held = [after(a, *gone) for a in mine[1:]]
        gone = tuple(send(a, dy=-dy) for dy, a in enumerate(held, 1))
        hold = loc_b[:, i * HD : (i + 1) * HD]
        if i > 0:
            hold = after(hold, before)
        att = finish(one, [mine[0], *gone], hold, queries, gate_rows)
        pieces += [(one, k, att if k == 0 else send_x(att, k)) for k in range(NX)]
    return project(source, pieces, out_weight, before, True)


def solution(mesh):
    placed = (
        P("mem", "blk"),
        P("mem", "blk"),
        P("mem", "blk"),
        P("mem", None, "blk"),
        P("mem", None, "blk"),
        P("mem", None),
        P("blk"),
        P(),
        P(None, "blk"),
    )
    return jax.shard_map(
        shards, mesh=mesh, in_specs=placed, out_specs=P("mem", "blk"), check_vma=False
    )
```

```python
import functools

import jax
import jax.numpy as jnp
from jax import lax
from jax.experimental import pallas as pl
from jax.experimental.pallas import tpu as pltpu
from jax.sharding import PartitionSpec as P

NY, NZ, NC, NX = 4, 8, 2, 4
HD = 128
BT = 128
TOK = 512
NH = 4
QB = 4
SLOTS = 4
EXTRA = 16
ROWS = HD + EXTRA
BF, F32 = jnp.bfloat16, jnp.float32
LOG2E = 1.4426950408889634
C2 = LOG2E * HD**-0.5
LOW = -1e30
MIB = 1024 * 1024
GROUPS = ((0, 2), (2, 2))


def send(block, dy=0, dz=0, dc=0):
    route = []
    for y in range(NY):
        for z in range(NZ):
            for c in range(NC):
                to = (((y + dy) % NY) * NZ + (z + dz) % NZ) * NC + (c + dc) % NC
                route.append(((y * NZ + z) * NC + c, to))
    return lax.ppermute(block, "mem", route)


def send_x(block, dx):
    return lax.ppermute(block, "blk", [(x, (x + dx) % NX) for x in range(NX)])


def nt(a, b):
    return lax.dot_general(a, b, (((1,), (1,)), ((), ())), preferred_element_type=F32)


def cost(flops, bytes_accessed, exps=0):
    return pl.CostEstimate(
        flops=int(flops), bytes_accessed=int(bytes_accessed), transcendentals=int(exps)
    )


def params(size=16):
    return pltpu.CompilerParams(vmem_limit_bytes=size * MIB)


def pack_kernel(k_ref, v_ref, *outs):
    for out, (head, n) in zip(outs, GROUPS):
        for i in range(n):
            cols = slice((head + i) * HD, (head + i + 1) * HD)
            for s in range(SLOTS):
                out[0, i, s] = k_ref[s, :, cols]
                out[1, i, s] = v_ref[s, :, cols].T


def pack(keys, values):
    return pl.pallas_call(
        pack_kernel,
        out_shape=[jax.ShapeDtypeStruct((2, n, SLOTS, BT, HD), BF) for _, n in GROUPS],
        name="pack",
        compiler_params=params(),
        cost_estimate=cost(0, 2**21),
    )(keys, values)


def gate_of(q, row):
    logit = jnp.sum(q.astype(F32) * row, axis=1, keepdims=True) * F32(HD**-0.5)
    return 1.0 / (1.0 + jnp.exp(-logit))


def local_kernel(first_ref, q_ref, kp_ref, ko_ref, vp_ref, vo_ref, g_ref, out_ref, k_all, v_all):
    k_all[:TOK] = kp_ref[...]
    k_all[TOK:] = ko_ref[...]
    v_all[:TOK] = vp_ref[...]
    v_all[TOK:] = vo_ref[...]
    start = first_ref[0]
    span = TOK + BT
    row = lax.broadcasted_iota(jnp.int32, (BT, span), 0)
    col = lax.broadcasted_iota(jnp.int32, (BT, span), 1)
    band = (col > row) & (col <= row + TOK)
    for b in range(QB):
        q = q_ref[b * BT : (b + 1) * BT]
        s = nt(q, k_all[b * BT : b * BT + span])
        s = jnp.where(band & (col + b * BT >= start), s, LOW)
        top = jnp.max(s, axis=1, keepdims=True)
        p = jnp.exp2((s - top) * C2)
        total = jnp.sum(p, axis=1, keepdims=True)
        o = jnp.dot(p.astype(BF), v_all[b * BT : b * BT + span], preferred_element_type=F32)
        gate = gate_of(q, g_ref[0])
        out_ref[b * BT : (b + 1) * BT] = o * ((1.0 - gate) / total)


def local(group, first, q, kp, ko, vp, vo, gate_rows):
    head, n = group
    spec = pl.BlockSpec((TOK, HD), lambda i: (0, head + i))
    return pl.pallas_call(
        local_kernel,
        out_shape=jax.ShapeDtypeStruct((TOK, n * HD), F32),
        grid=(n,),
        in_specs=[pl.BlockSpec(memory_space=pltpu.SMEM)]
        + [spec] * 5
        + [pl.BlockSpec((1, 1, HD), lambda i: (head + i, 0, 0))],
        out_specs=pl.BlockSpec((TOK, HD), lambda i: (0, i)),
        scratch_shapes=[pltpu.VMEM((2 * TOK, HD), BF)] * 2,
        name="local",
        compiler_params=params(),
        cost_estimate=cost(n * 4 * TOK * 640 * HD, n * 2**20, n * TOK * 640),
    )(first, q, kp, ko, vp, vo, gate_rows)


def write_part(ref, where, value, lse):
    ref[(*where, pl.ds(0, HD))] = value.astype(BF)
    hi = lse.astype(BF)
    rest = lse - hi.astype(F32)
    mid = rest.astype(BF)
    lo = (rest - mid.astype(F32)).astype(BF)
    n = lax.broadcasted_iota(jnp.int32, (EXTRA, BT), 0)
    tail = jnp.where(
        n == 0,
        hi.astype(F32),
        jnp.where(n == 1, mid.astype(F32), jnp.where(n == 2, lo.astype(F32), 0.0)),
    )
    ref[(*where, pl.ds(HD, EXTRA))] = tail.astype(BF)


def read_part(ref, where):
    tail = ref[(*where, pl.ds(HD, EXTRA))].astype(F32)
    return ref[(*where, pl.ds(0, HD))].astype(F32), jnp.sum(tail, axis=0, keepdims=True)


def mem_kernel(n, table, *refs):
    qs, ks, vs, outs, accs = refs[:2], refs[2:18:2], refs[3:18:2], refs[18:20], refs[20]

    def one(dy, carry):
        for dc in range(NC):
            entry = [table[dc, dy, o] for o in range(NZ)]
            valid = [e > 0 for e in entry]
            place = [jnp.maximum(e - 1, 0) for e in entry]
            block = [p // SLOTS for p in place]
            slot = [p % SLOTS for p in place]
            for i in range(n):
                acc = accs.at[dc * n + i]
                scores, tops = [], []
                for o in range(NZ):
                    q = qs[dc][
                        dy, pl.ds(pl.multiple_of(block[o] * BT, BT), BT), i * HD : (i + 1) * HD
                    ]
                    s = nt(ks[o][0, i, slot[o]], q)
                    scores.append(s)
                    tops.append(jnp.max(s, axis=0, keepdims=True))
                top = []
                for b in range(QB):
                    best = jnp.full((1, BT), LOW, F32)
                    for o in range(NZ):
                        here = valid[o] & (block[o] == b)
                        best = jnp.maximum(best, jnp.where(here, tops[o], LOW))
                    top.append(best)
                acc[...] = jnp.zeros_like(acc)
                total = [jnp.zeros((1, BT), F32) for _ in range(QB)]
                for o in range(NZ):
                    mine = jnp.full((1, BT), -LOW, F32)
                    for b in range(QB):
                        mine = jnp.where(valid[o] & (block[o] == b), top[b], mine)
                    p = jnp.exp2((scores[o] - mine) * C2)
                    size = jnp.sum(p, axis=0, keepdims=True)
                    for b in range(QB):
                        total[b] += jnp.where(block[o] == b, size, 0.0)
                    acc[block[o]] += jnp.dot(
                        vs[o][0, i, slot[o]], p.astype(BF), preferred_element_type=F32
                    )
                for b in range(QB):
                    some = total[b] > 0
                    safe = jnp.where(some, total[b], 1.0)
                    lse = jnp.where(some, top[b] * C2 + jnp.log2(safe), LOW)
                    write_part(outs[dc], (dy, i, b), acc[b] * (1.0 / safe), lse)
        return carry

    lax.fori_loop(0, NY, one, 0)


def mem_attention(group, table, qa, qb, kvs):
    head, n = group
    part = jax.ShapeDtypeStruct((NY, n, QB, ROWS, BT), BF)
    qspec = pl.BlockSpec((NY, TOK, n * HD), lambda i: (0, 0, head // n))
    operands, specs = [], []
    for array, index in kvs:
        operands.append(array)
        specs.append(
            pl.BlockSpec((1, n, SLOTS, BT, HD), lambda i, index=index: (index, 0, 0, 0, 0))
        )
    out = pl.BlockSpec((NY, n, QB, ROWS, BT), lambda i: (0, 0, 0, 0, 0))
    return pl.pallas_call(
        functools.partial(mem_kernel, n),
        out_shape=[part] * NC,
        grid=(1,),
        in_specs=[pl.BlockSpec(memory_space=pltpu.SMEM)] + [qspec] * 2 + specs,
        out_specs=[out] * NC,
        scratch_shapes=[pltpu.VMEM((NC * n, QB, HD, BT), F32)],
        name="memory",
        compiler_params=params(26),
        cost_estimate=cost(n * 64 * 4 * BT * BT * HD, n * 5 * 2**20, n * 64 * BT * BT),
    )(table, qa, qb, *operands)


def merged(parts):
    values = [v for v, _ in parts]
    tops = [t for _, t in parts]
    best = functools.reduce(jnp.maximum, tops)
    weights = [jnp.exp2(t - best) for t in tops]
    total = sum(weights)
    share = 1.0 / total
    return sum(v * (w * share) for v, w in zip(values, weights)), best + jnp.log2(total)


def pair_kernel(n, a_ref, *refs):
    others, outs = refs[: NY * n], refs[NY * n :]
    for dy in range(NY):
        for i in range(n):
            for b in range(QB):
                both = [read_part(a_ref, (dy, i, b)), read_part(others[dy * n + i], (b,))]
                value, lse = merged(both)
                write_part(outs[dy], (i, b), value, lse)


def pair(group, a, b):
    n = group[1]
    others = [send(b[dy, i], dc=1) for dy in range(NY) for i in range(n)]
    return pl.pallas_call(
        functools.partial(pair_kernel, n),
        out_shape=[jax.ShapeDtypeStruct((n, QB, ROWS, BT), BF)] * NY,
        name="pair",
        compiler_params=params(),
        cost_estimate=cost(n * 2**21, n * 2**21),
    )(a, *others)


def finish_kernel(p0, p1, p2, p3, loc_ref, q_ref, g_ref, out_ref):
    for b in range(QB):
        value, _ = merged([read_part(p, (0, b)) for p in (p0, p1, p2, p3)])
        rows = slice(b * BT, (b + 1) * BT)
        gate = gate_of(q_ref[rows], g_ref[0])
        out_ref[rows] = (gate * value.T + loc_ref[rows]).astype(BF)


def finish(group, parts, loc, q, gate_rows):
    head, n = group
    part = pl.BlockSpec((1, QB, ROWS, BT), lambda i: (i, 0, 0, 0))
    return pl.pallas_call(
        finish_kernel,
        out_shape=jax.ShapeDtypeStruct((TOK, n * HD), BF),
        grid=(n,),
        in_specs=[part] * 4
        + [
            pl.BlockSpec((TOK, HD), lambda i: (0, i)),
            pl.BlockSpec((TOK, HD), lambda i: (0, head + i)),
            pl.BlockSpec((1, 1, HD), lambda i: (head + i, 0, 0)),
        ],
        out_specs=pl.BlockSpec((TOK, HD), lambda i: (0, i)),
        name="finish",
        compiler_params=params(),
        cost_estimate=cost(n * 2**20, n * 2**20),
    )(*parts, loc, q, gate_rows)


def project_kernel(n, source, *refs):
    atts, weights, rest = refs[:n], refs[n : 2 * n], refs[2 * n :]
    total = rest[0][...] if len(rest) == 2 else None
    for a, w in zip(atts, weights):
        term = jnp.dot(a[...], w[...], preferred_element_type=F32)
        total = term if total is None else total + term
    rest[-1][...] = total.astype(rest[-1].dtype)


def project(source, pieces, out_weight, before, last):
    m = len(pieces)
    width = out_weight.shape[1]
    tile = 512

    def weight_spec(group, k):
        head, n = group
        return pl.BlockSpec((n * HD, tile), lambda i, src: ((src[k] * NH + head) // n, i))

    acc = pl.BlockSpec((TOK, tile), lambda i, src: (0, i))
    in_specs = [pl.BlockSpec((TOK, g[1] * HD), lambda i, src: (0, 0)) for g, _, _ in pieces]
    in_specs += [weight_spec(g, k) for g, k, _ in pieces]
    operands = [a for _, _, a in pieces] + [out_weight] * m
    if before is not None:
        in_specs.append(acc)
        operands.append(before)
    depth = sum(g[1] for g, _, _ in pieces) * HD
    return pl.pallas_call(
        functools.partial(project_kernel, m),
        out_shape=jax.ShapeDtypeStruct((TOK, width), BF if last else F32),
        grid_spec=pltpu.PrefetchScalarGridSpec(
            num_scalar_prefetch=1,
            grid=(width // tile,),
            in_specs=in_specs,
            out_specs=acc,
        ),
        name="project",
        compiler_params=params(),
        cost_estimate=cost(2 * TOK * depth * width, 6 * 2**20),
    )(source, *operands)


def after(block, *others):
    return lax.optimization_barrier((block, *others))[0]


def step(chain, dz, *others):
    chain.append(send(after(chain[-1], *others) if others else chain[-1], dz=dz))


def shards(
    queries,
    local_keys,
    local_values,
    memory_keys,
    memory_values,
    block_ids,
    gate_index,
    gate_vectors,
    out_weight,
):
    me = lax.axis_index("mem")
    y, z, c = me // (NZ * NC), (me // NC) % NZ, me % NC
    x = lax.axis_index("blk")
    kv = pack(memory_keys, memory_values)

    wanted = block_ids.size
    note = jnp.pad(block_ids.reshape(1, -1).astype(BF), ((0, EXTRA - 1), (0, NH * HD - wanted)))
    ga, gb = GROUPS
    up_a, down_a = [kv[0]], [kv[0]]
    step(up_a, 1)
    step(down_a, -1)
    noted = after(jnp.concatenate([queries, note]), up_a[1])
    near = [noted, send(noted, dy=1), send(noted, dy=2), send(noted, dy=3)]
    route = [(i, i + 1) for i in range(NY * NZ * NC - 1)]
    kp = lax.ppermute(local_keys, "mem", route)
    vp = lax.ppermute(local_values, "mem", route)
    first = jnp.where(me > 0, 0, TOK).astype(jnp.int32)[None]
    which = gate_index[:, None] == jnp.arange(gate_vectors.shape[0], dtype=jnp.int32)[None, :]
    gate_rows = jnp.sum(jnp.where(which[:, :, None], gate_vectors[None], 0.0), axis=1)[:, None, :]
    source = ((x - jnp.arange(NX, dtype=jnp.int32)) % NX).astype(jnp.int32)
    step(up_a, 1)
    step(down_a, -1)
    loc_a = local(ga, first, queries, kp, local_keys, vp, local_values, gate_rows)
    loc_b = local(gb, first, queries, kp, local_keys, vp, local_values, gate_rows)
    up_b, down_b = [after(kv[1], up_a[2], loc_a)], [after(kv[1], down_a[2], loc_a)]
    step(up_a, 1)
    step(down_a, -1)
    step(up_b, 1)
    step(down_b, -1)
    near = [after(q, up_b[1], down_b[1]) for q in near]
    qa = jnp.stack(near)
    qb = jnp.stack([send(q, dc=1) for q in near])
    ids = jnp.stack([qa[:, TOK, :wanted], qb[:, TOK, :wanted]]).astype(jnp.int32)
    owners = (y * NZ + (z - jnp.arange(NZ, dtype=jnp.int32)) % NZ) * NC + c
    position = jnp.arange(wanted, dtype=jnp.int32) // block_ids.shape[1]
    code = 1 + position * SLOTS + ids % SLOTS
    hit = (ids // SLOTS)[:, :, None, :] == owners[None, None, :, None]
    table = jnp.sum(jnp.where(hit, code[:, :, None, :], 0), axis=-1)

    step(down_a, -1, loc_b)
    step(up_b, 1)
    step(down_b, -1)
    step(up_b, 1)
    step(down_b, -1)
    kvs = [(a, j) for a in up_a + down_a[:0:-1] for j in range(2)]
    pa, pb = mem_attention(ga, table, qa, qb, kvs)
    far = [(send(after(up_b[3], pa)[:1], dz=1), 0), (send(after(down_b[3], pa)[1:], dz=-1), 0)]
    m = pair(ga, pa, pb)
    parts = [m[0], send(m[1], dy=-1), send(m[2], dy=-2), send(m[3], dy=-3)]
    att_a = finish(ga, parts, loc_a, queries, gate_rows)
    pieces = [(ga, k, att_a if k == 0 else send_x(att_a, k)) for k in range(NX)]
    before = project(source, pieces, out_weight, None, False)

    kvs = [(a, j) for a in up_b for j in range(2)] + far
    kvs += [(a, j) for a in down_b[:0:-1] for j in range(2)]
    pa, pb = mem_attention(gb, after(table, m[0]), qa, qb, kvs)
    m = pair(gb, after(pa, att_a), pb)
    parts = [m[0], send(m[1], dy=-1), send(m[2], dy=-2), send(m[3], dy=-3)]
    att = finish(gb, parts, after(loc_b, before), queries, gate_rows)
    pieces = [(gb, k, att if k == 0 else send_x(att, k)) for k in range(NX)]
    return project(source, pieces, out_weight, before, True)


def solution(mesh):
    placed = (
        P("mem", "blk"),
        P("mem", "blk"),
        P("mem", "blk"),
        P("mem", None, "blk"),
        P("mem", None, "blk"),
        P("mem", None),
        P("blk"),
        P(),
        P(None, "blk"),
    )
    return jax.shard_map(
        shards, mesh=mesh, in_specs=placed, out_specs=P("mem", "blk"), check_vma=False
    )
```

```python
import functools

import jax
import jax.numpy as jnp
from jax import lax
from jax.experimental import pallas as pl
from jax.experimental.pallas import tpu as pltpu
from jax.sharding import PartitionSpec as P

NY, NZ, NC, NX = 4, 8, 2, 4
HD = 128
BT = 128
TOK = 512
NH = 4
QB = 4
SLOTS = 4
EXTRA = 16
ROWS = HD + EXTRA
BF, F32 = jnp.bfloat16, jnp.float32
LOG2E = 1.4426950408889634
C2 = LOG2E * HD**-0.5
LOW = -1e30
MIB = 1024 * 1024
GROUPS = ((0, 2), (2, 2))


def send(block, dy=0, dz=0, dc=0):
    route = []
    for y in range(NY):
        for z in range(NZ):
            for c in range(NC):
                to = (((y + dy) % NY) * NZ + (z + dz) % NZ) * NC + (c + dc) % NC
                route.append(((y * NZ + z) * NC + c, to))
    return lax.ppermute(block, "mem", route)


def send_x(block, dx):
    return lax.ppermute(block, "blk", [(x, (x + dx) % NX) for x in range(NX)])


def nt(a, b):
    return lax.dot_general(a, b, (((1,), (1,)), ((), ())), preferred_element_type=F32)


def cost(flops, bytes_accessed, exps=0):
    return pl.CostEstimate(
        flops=int(flops), bytes_accessed=int(bytes_accessed), transcendentals=int(exps)
    )


def params(size=16):
    return pltpu.CompilerParams(vmem_limit_bytes=size * MIB)


def pack_kernel(k_ref, v_ref, *outs):
    for out, (head, n) in zip(outs, GROUPS):
        for i in range(n):
            cols = slice((head + i) * HD, (head + i + 1) * HD)
            for s in range(SLOTS):
                out[0, i, s] = k_ref[s, :, cols]
                out[1, i, s] = v_ref[s, :, cols].T


def pack(keys, values):
    return pl.pallas_call(
        pack_kernel,
        out_shape=[jax.ShapeDtypeStruct((2, n, SLOTS, BT, HD), BF) for _, n in GROUPS],
        name="pack",
        compiler_params=params(),
        cost_estimate=cost(0, 2**21),
    )(keys, values)


def gate_of(q, row):
    logit = jnp.sum(q.astype(F32) * row, axis=1, keepdims=True) * F32(HD**-0.5)
    return 1.0 / (1.0 + jnp.exp(-logit))


def local_kernel(first_ref, q_ref, kp_ref, ko_ref, vp_ref, vo_ref, g_ref, out_ref, k_all, v_all):
    k_all[:TOK] = kp_ref[...]
    k_all[TOK:] = ko_ref[...]
    v_all[:TOK] = vp_ref[...]
    v_all[TOK:] = vo_ref[...]
    start = first_ref[0]
    span = TOK + BT
    row = lax.broadcasted_iota(jnp.int32, (BT, span), 0)
    col = lax.broadcasted_iota(jnp.int32, (BT, span), 1)
    band = (col > row) & (col <= row + TOK)
    for b in range(QB):
        q = q_ref[b * BT : (b + 1) * BT]
        s = nt(q, k_all[b * BT : b * BT + span])
        s = jnp.where(band & (col + b * BT >= start), s, LOW)
        top = jnp.max(s, axis=1, keepdims=True)
        p = jnp.exp2((s - top) * C2)
        total = jnp.sum(p, axis=1, keepdims=True)
        o = jnp.dot(p.astype(BF), v_all[b * BT : b * BT + span], preferred_element_type=F32)
        gate = gate_of(q, g_ref[0])
        out_ref[b * BT : (b + 1) * BT] = o * ((1.0 - gate) / total)


def local(group, first, q, kp, ko, vp, vo, gate_rows):
    head, n = group
    spec = pl.BlockSpec((TOK, HD), lambda i: (0, head + i))
    return pl.pallas_call(
        local_kernel,
        out_shape=jax.ShapeDtypeStruct((TOK, n * HD), F32),
        grid=(n,),
        in_specs=[pl.BlockSpec(memory_space=pltpu.SMEM)]
        + [spec] * 5
        + [pl.BlockSpec((1, 1, HD), lambda i: (head + i, 0, 0))],
        out_specs=pl.BlockSpec((TOK, HD), lambda i: (0, i)),
        scratch_shapes=[pltpu.VMEM((2 * TOK, HD), BF)] * 2,
        name="local",
        compiler_params=params(),
        cost_estimate=cost(n * 4 * TOK * 640 * HD, n * 2**20, n * TOK * 640),
    )(first, q, kp, ko, vp, vo, gate_rows)


def write_part(ref, where, value, lse):
    ref[(*where, pl.ds(0, HD))] = value.astype(BF)
    hi = lse.astype(BF)
    rest = lse - hi.astype(F32)
    mid = rest.astype(BF)
    lo = (rest - mid.astype(F32)).astype(BF)
    n = lax.broadcasted_iota(jnp.int32, (EXTRA, BT), 0)
    tail = jnp.where(
        n == 0,
        hi.astype(F32),
        jnp.where(n == 1, mid.astype(F32), jnp.where(n == 2, lo.astype(F32), 0.0)),
    )
    ref[(*where, pl.ds(HD, EXTRA))] = tail.astype(BF)


def read_part(ref, where):
    tail = ref[(*where, pl.ds(HD, EXTRA))].astype(F32)
    return ref[(*where, pl.ds(0, HD))].astype(F32), jnp.sum(tail, axis=0, keepdims=True)


def mem_kernel(n, table, *refs):
    qs, ks, vs, outs, accs = refs[:2], refs[2:18:2], refs[3:18:2], refs[18:20], refs[20]

    def one(dy, carry):
        for dc in range(NC):
            entry = [table[dc, dy, o] for o in range(NZ)]
            valid = [e > 0 for e in entry]
            place = [jnp.maximum(e - 1, 0) for e in entry]
            block = [p // SLOTS for p in place]
            slot = [p % SLOTS for p in place]
            for i in range(n):
                acc = accs.at[dc * n + i]
                scores, tops = [], []
                for o in range(NZ):
                    q = qs[dc][
                        dy, pl.ds(pl.multiple_of(block[o] * BT, BT), BT), i * HD : (i + 1) * HD
                    ]
                    s = nt(ks[o][0, i, slot[o]], q)
                    scores.append(s)
                    tops.append(jnp.max(s, axis=0, keepdims=True))
                top = []
                for b in range(QB):
                    best = jnp.full((1, BT), LOW, F32)
                    for o in range(NZ):
                        here = valid[o] & (block[o] == b)
                        best = jnp.maximum(best, jnp.where(here, tops[o], LOW))
                    top.append(best)
                acc[...] = jnp.zeros_like(acc)
                total = [jnp.zeros((1, BT), F32) for _ in range(QB)]
                for o in range(NZ):
                    mine = jnp.full((1, BT), -LOW, F32)
                    for b in range(QB):
                        mine = jnp.where(valid[o] & (block[o] == b), top[b], mine)
                    p = jnp.exp2((scores[o] - mine) * C2)
                    size = jnp.sum(p, axis=0, keepdims=True)
                    for b in range(QB):
                        total[b] += jnp.where(block[o] == b, size, 0.0)
                    acc[block[o]] += jnp.dot(
                        vs[o][0, i, slot[o]], p.astype(BF), preferred_element_type=F32
                    )
                for b in range(QB):
                    some = total[b] > 0
                    safe = jnp.where(some, total[b], 1.0)
                    lse = jnp.where(some, top[b] * C2 + jnp.log2(safe), LOW)
                    write_part(outs[dc], (dy, i, b), acc[b] * (1.0 / safe), lse)
        return carry

    lax.fori_loop(0, NY, one, 0)


def mem_attention(group, table, qa, qb, kvs):
    head, n = group
    part = jax.ShapeDtypeStruct((NY, n, QB, ROWS, BT), BF)
    qspec = pl.BlockSpec((NY, TOK, n * HD), lambda i: (0, 0, head // n))
    operands, specs = [], []
    for array, index in kvs:
        operands.append(array)
        specs.append(
            pl.BlockSpec((1, n, SLOTS, BT, HD), lambda i, index=index: (index, 0, 0, 0, 0))
        )
    out = pl.BlockSpec((NY, n, QB, ROWS, BT), lambda i: (0, 0, 0, 0, 0))
    return pl.pallas_call(
        functools.partial(mem_kernel, n),
        out_shape=[part] * NC,
        grid=(1,),
        in_specs=[pl.BlockSpec(memory_space=pltpu.SMEM)] + [qspec] * 2 + specs,
        out_specs=[out] * NC,
        scratch_shapes=[pltpu.VMEM((NC * n, QB, HD, BT), F32)],
        name="memory",
        compiler_params=params(26),
        cost_estimate=cost(n * 64 * 4 * BT * BT * HD, n * 5 * 2**20, n * 64 * BT * BT),
    )(table, qa, qb, *operands)


def merged(parts):
    values = [v for v, _ in parts]
    tops = [t for _, t in parts]
    best = functools.reduce(jnp.maximum, tops)
    weights = [jnp.exp2(t - best) for t in tops]
    total = sum(weights)
    share = 1.0 / total
    return sum(v * (w * share) for v, w in zip(values, weights)), best + jnp.log2(total)


def pair_kernel(n, a_ref, *refs):
    others, outs = refs[: NY * n], refs[NY * n :]
    for dy in range(NY):
        for i in range(n):
            for b in range(QB):
                both = [read_part(a_ref, (dy, i, b)), read_part(others[dy * n + i], (b,))]
                value, lse = merged(both)
                write_part(outs[dy], (i, b), value, lse)


def pair(group, a, b):
    n = group[1]
    others = [send(b[dy, i], dc=1) for dy in range(NY) for i in range(n)]
    return pl.pallas_call(
        functools.partial(pair_kernel, n),
        out_shape=[jax.ShapeDtypeStruct((n, QB, ROWS, BT), BF)] * NY,
        name="pair",
        compiler_params=params(),
        cost_estimate=cost(n * 2**21, n * 2**21),
    )(a, *others)


def finish_kernel(p0, p1, p2, p3, loc_ref, q_ref, g_ref, out_ref):
    for b in range(QB):
        value, _ = merged([read_part(p, (0, b)) for p in (p0, p1, p2, p3)])
        rows = slice(b * BT, (b + 1) * BT)
        gate = gate_of(q_ref[rows], g_ref[0])
        out_ref[rows] = (gate * value.T + loc_ref[rows]).astype(BF)


def finish(group, parts, loc, q, gate_rows):
    head, n = group
    part = pl.BlockSpec((1, QB, ROWS, BT), lambda i: (i, 0, 0, 0))
    return pl.pallas_call(
        finish_kernel,
        out_shape=jax.ShapeDtypeStruct((TOK, n * HD), BF),
        grid=(n,),
        in_specs=[part] * 4
        + [
            pl.BlockSpec((TOK, HD), lambda i: (0, i)),
            pl.BlockSpec((TOK, HD), lambda i: (0, head + i)),
            pl.BlockSpec((1, 1, HD), lambda i: (head + i, 0, 0)),
        ],
        out_specs=pl.BlockSpec((TOK, HD), lambda i: (0, i)),
        name="finish",
        compiler_params=params(),
        cost_estimate=cost(n * 2**20, n * 2**20),
    )(*parts, loc, q, gate_rows)


def project_kernel(n, source, *refs):
    atts, weights, rest = refs[:n], refs[n : 2 * n], refs[2 * n :]
    total = rest[0][...] if len(rest) == 2 else None
    for a, w in zip(atts, weights):
        term = jnp.dot(a[...], w[...], preferred_element_type=F32)
        total = term if total is None else total + term
    rest[-1][...] = total.astype(rest[-1].dtype)


def project(source, pieces, out_weight, before, last):
    m = len(pieces)
    width = out_weight.shape[1]
    tile = 256

    def weight_spec(group, k):
        head, n = group
        return pl.BlockSpec((n * HD, tile), lambda i, src: ((src[k] * NH + head) // n, i))

    acc = pl.BlockSpec((TOK, tile), lambda i, src: (0, i))
    in_specs = [pl.BlockSpec((TOK, g[1] * HD), lambda i, src: (0, 0)) for g, _, _ in pieces]
    in_specs += [weight_spec(g, k) for g, k, _ in pieces]
    operands = [a for _, _, a in pieces] + [out_weight] * m
    if before is not None:
        in_specs.append(acc)
        operands.append(before)
    depth = sum(g[1] for g, _, _ in pieces) * HD
    return pl.pallas_call(
        functools.partial(project_kernel, m),
        out_shape=jax.ShapeDtypeStruct((TOK, width), BF if last else F32),
        grid_spec=pltpu.PrefetchScalarGridSpec(
            num_scalar_prefetch=1,
            grid=(width // tile,),
            in_specs=in_specs,
            out_specs=acc,
        ),
        name="project",
        compiler_params=params(),
        cost_estimate=cost(2 * TOK * depth * width, 6 * 2**20),
    )(source, *operands)


def after(block, *others):
    return lax.optimization_barrier((block, *others))[0]


def step(chain, dz, *others):
    chain.append(send(after(chain[-1], *others) if others else chain[-1], dz=dz))


def shards(
    queries,
    local_keys,
    local_values,
    memory_keys,
    memory_values,
    block_ids,
    gate_index,
    gate_vectors,
    out_weight,
):
    me = lax.axis_index("mem")
    y, z, c = me // (NZ * NC), (me // NC) % NZ, me % NC
    x = lax.axis_index("blk")
    kv = pack(memory_keys, memory_values)

    wanted = block_ids.size
    note = jnp.pad(block_ids.reshape(1, -1).astype(BF), ((0, EXTRA - 1), (0, NH * HD - wanted)))
    ga, gb = GROUPS
    up_a, down_a = [kv[0]], [kv[0]]
    step(up_a, 1)
    step(down_a, -1)
    noted = after(jnp.concatenate([queries, note]), up_a[1])
    near = [noted, send(noted, dy=1), send(noted, dy=2), send(noted, dy=3)]
    route = [(i, i + 1) for i in range(NY * NZ * NC - 1)]
    kp = lax.ppermute(local_keys, "mem", route)
    vp = lax.ppermute(local_values, "mem", route)
    first = jnp.where(me > 0, 0, TOK).astype(jnp.int32)[None]
    which = gate_index[:, None] == jnp.arange(gate_vectors.shape[0], dtype=jnp.int32)[None, :]
    gate_rows = jnp.sum(jnp.where(which[:, :, None], gate_vectors[None], 0.0), axis=1)[:, None, :]
    source = ((x - jnp.arange(NX, dtype=jnp.int32)) % NX).astype(jnp.int32)
    step(up_a, 1)
    step(down_a, -1)
    loc_a = local(ga, first, queries, kp, local_keys, vp, local_values, gate_rows)
    loc_b = local(gb, first, queries, kp, local_keys, vp, local_values, gate_rows)
    up_b, down_b = [after(kv[1], up_a[2], loc_a)], [after(kv[1], down_a[2], loc_a)]
    step(up_a, 1)
    step(down_a, -1)
    step(up_b, 1)
    step(down_b, -1)
    near = [after(q, up_b[1], down_b[1]) for q in near]
    qa = jnp.stack(near)
    qb = jnp.stack([send(q, dc=1) for q in near])
    ids = jnp.stack([qa[:, TOK, :wanted], qb[:, TOK, :wanted]]).astype(jnp.int32)
    owners = (y * NZ + (z - jnp.arange(NZ, dtype=jnp.int32)) % NZ) * NC + c
    position = jnp.arange(wanted, dtype=jnp.int32) // block_ids.shape[1]
    code = 1 + position * SLOTS + ids % SLOTS
    hit = (ids // SLOTS)[:, :, None, :] == owners[None, None, :, None]
    table = jnp.sum(jnp.where(hit, code[:, :, None, :], 0), axis=-1)

    step(down_a, -1, loc_b)
    step(up_b, 1)
    step(down_b, -1)
    step(up_b, 1)
    step(down_b, -1)
    kvs = [(a, j) for a in up_a + down_a[:0:-1] for j in range(2)]
    pa, pb = mem_attention(ga, table, qa, qb, kvs)
    far = [(send(after(up_b[3], pa)[:1], dz=1), 0), (send(after(down_b[3], pa)[1:], dz=-1), 0)]
    m = pair(ga, pa, pb)
    parts = [m[0], send(m[1], dy=-1), send(m[2], dy=-2), send(m[3], dy=-3)]
    att_a = finish(ga, parts, loc_a, queries, gate_rows)
    pieces = [(ga, k, att_a if k == 0 else send_x(att_a, k)) for k in range(NX)]
    before = project(source, pieces, out_weight, None, False)

    kvs = [(a, j) for a in up_b for j in range(2)] + far
    kvs += [(a, j) for a in down_b[:0:-1] for j in range(2)]
    pa, pb = mem_attention(gb, after(table, m[0]), qa, qb, kvs)
    m = pair(gb, after(pa, att_a), pb)
    parts = [m[0], send(m[1], dy=-1), send(m[2], dy=-2), send(m[3], dy=-3)]
    att = finish(gb, parts, after(loc_b, before), queries, gate_rows)
    pieces = [(gb, k, att if k == 0 else send_x(att, k)) for k in range(NX)]
    return project(source, pieces, out_weight, before, True)


def solution(mesh):
    placed = (
        P("mem", "blk"),
        P("mem", "blk"),
        P("mem", "blk"),
        P("mem", None, "blk"),
        P("mem", None, "blk"),
        P("mem", None),
        P("blk"),
        P(),
        P(None, "blk"),
    )
    return jax.shard_map(
        shards, mesh=mesh, in_specs=placed, out_specs=P("mem", "blk"), check_vma=False
    )
```
